32 devices in a mesh: groups: 2 (over y), seq: 4 (over z), mp: 2 (over x), pipe: 2 (over core).
Axes of the slice: x: 2, y: 2, z: 4, core: 2. Of those that a mesh axis runs over, the one named last changes fastest.
Arguments:
- query: bfloat16 [16384, 1024], P(('groups', 'seq', 'pipe'), 'mp'), parts along dimension 0, may hold values from -6 to 6
- key_in: bfloat16 [16384, 1024], P(('groups', 'seq', 'pipe'), 'mp'), parts along dimension 0, may hold values from -6 to 6
- value_in: bfloat16 [16384, 1024], P(('groups', 'seq', 'pipe'), 'mp'), parts along dimension 0, may hold values from -6 to 6
- gate_u: bfloat16 [16384, 1024], P(('groups', 'seq', 'pipe'), 'mp'), parts along dimension 0, may hold values from -6 to 6
- grad_out: bfloat16 [16384, 1024], P(('groups', 'seq', 'pipe'), 'mp'), parts along dimension 0, may hold values from -6 to 6
- segment_ids: int32 [16384], P('groups'), parts along dimension 0, may hold values from 0 to 95, never falling along the last dimension, each value on 1 to 256 neighbouring positions
- sample_slot: int32 [16384], P(('groups', 'seq', 'pipe')), parts along dimension 0, may hold values from -1 to 511, as said below
- owned_input: bfloat16 [8192, 1024], P(('groups', 'seq')), parts along dimension 0, may hold values from -6 to 6
- task_grad: float32 [8192, 4], P(('groups', 'seq')), parts along dimension 0, may hold values from -6 to 6
- w_in: bfloat16 [4, 1024, 512], P(('mp', 'pipe')), may hold values from -0.1875 to 0.1875
- w_out: bfloat16 [4, 512, 256], P(('mp', 'pipe')), may hold values from -0.25 to 0.25
- w_gate: bfloat16 [4, 1024, 4], P(('mp', 'pipe')), may hold values from -0.1875 to 0.1875
- tower: bfloat16 [4, 256], replicated, may hold values from -6 to 6
Outputs:
- grad_q: bfloat16 [16384, 1024], P(('groups', 'seq', 'pipe'), 'mp'), parts along dimension 0
- grad_k: bfloat16 [16384, 1024], P(('groups', 'seq', 'pipe'), 'mp'), parts along dimension 0
- grad_v: bfloat16 [16384, 1024], P(('groups', 'seq', 'pipe'), 'mp'), parts along dimension 0
- grad_u: bfloat16 [16384, 1024], P(('groups', 'seq', 'pipe'), 'mp'), parts along dimension 0
The draws below stay inside these ranges and needn't reach their ends.
There are 2 independent parts, one for each index of `groups`. The reference program is written for one: setup_inputs(seed, part) draws one part's arguments, and reference() takes and returns one part's arrays. A program takes and returns all parts, laid end to end along the dimension named above; an argument that names none is the same for every part. Nothing has to cross between parts.
Inputs may be any that keep to these rules, and one draw needn't show every extreme that they name: `segment_ids`: A user's events are consecutive rows: the ids never fall along the rows, every user has at most 256 events and some user exactly 256. `sample_slot`: rows whose value is -1 carry no sample. Within one block of 1024 rows no value other than -1 appears twice. In every draw some owner receives all 128 slots from every block.
All inputs are finite; a program needn't handle non-finite values.
Results may differ from the reference program's by a relative error of at most 0.0062.
Values may be sent and summed in bfloat16 or wider, within the bound.
A program may use at most 128 MiB of HBM per device.

```python
import math
import jax
import jax.numpy as jnp
import numpy as np
from jax import lax

D = 1024
HEADS = 8
HDIM = 128
TASKS = 4
EH = 512
EO = 256
EXPERTS = 4
TOK_DEV = 1024
MOST = 256
BLOCKS = 8
OWNERS = 4
ROWS_OWNER = 1024
SLOTS = 128
TOKENS = 8192
USERS = 96
OWNED = 4096


def draw_sample_slot(key, part):
    key = jax.random.fold_in(key, 7)
    n_blocks = BLOCKS
    n_slots = OWNERS * SLOTS
    key_parts = jax.random.split(key, 5)
    full_owner = jax.random.randint(key_parts[0], (), 0, OWNERS)
    last_block = jax.random.randint(key_parts[1], (), 0, n_blocks)
    fill_level = jax.random.randint(key_parts[2], (n_blocks, 1), 1, 5)
    coin_draw = jax.random.randint(key_parts[3], (n_blocks, n_slots), 0, 4)
    slot_ids = jnp.arange(n_slots, dtype=jnp.int32)[None, :]
    block_ids = jnp.arange(n_blocks, dtype=jnp.int32)[:, None]
    in_use = (coin_draw < fill_level) | (slot_ids // SLOTS == full_owner) | (slot_ids == n_slots - 1) & (block_ids == last_block)
    slot_rank = jnp.cumsum(in_use.astype(jnp.int32), axis=1) - 1
    row_keys = jax.random.split(key_parts[4], n_blocks)
    orders = jax.vmap(lambda one_key: jax.random.permutation(one_key, TOK_DEV))(row_keys).astype(jnp.int32)
    target = jnp.take_along_axis(orders, jnp.maximum(slot_rank, 0), axis=1)
    target = jnp.where(in_use, target, TOK_DEV)
    slot_table = jnp.full((n_blocks, TOK_DEV + 1), -1, dtype=jnp.int32)
    slot_table = slot_table.at[jnp.broadcast_to(block_ids, (n_blocks, n_slots)), target].set(jnp.broadcast_to(slot_ids, (n_blocks, n_slots)))
    return slot_table[:, :TOK_DEV].reshape(n_blocks * TOK_DEV)


def levels(rng, dims, cuts, least, top_value):
    level = 1.0
    for axis_at, blocks in cuts:
        heights = jax.random.uniform(jax.random.fold_in(jax.random.fold_in(rng, 6), axis_at), (blocks,), jnp.float32, least / len(cuts), top_value / len(cuts))
        level = level * jnp.repeat(jnp.exp(heights), dims[axis_at] // blocks).reshape((-1,) + (1,) * (len(dims) - 1 - axis_at))
    return level


def profile(count, total, most, lean):
    loads = [(1 << 20) // math.isqrt(grade ** lean) + 1 for grade in range(2, count + 1)]
    rest, counts = total - most - (count - 1), [1] * (count - 1)
    while rest > 0:
        candidates = [i for i in range(count - 1) if counts[i] < most]
        pool, budget = sum([loads[i] for i in candidates]), rest
        for i in candidates:
            extra = min(most - counts[i], max(1, budget * loads[i] // pool), rest)
            counts[i] = counts[i] + extra
            rest = rest - extra
    return np.array([most] + counts)


def uneven(key, amount, total, limit, lean):
    if amount == 2:
        one = jax.random.randint(key, (), max(1, total - limit), min(limit, total - 1) + 1)
        return jnp.stack([one, total - one])
    tallies = jnp.asarray(profile(amount, total, limit, lean), jnp.int32)
    couples = (amount - 1) // 2
    source_of, sink = tallies[1:1 + 2 * couples:2], tallies[2:2 + 2 * couples:2]
    margin = jnp.minimum(source_of - 1, limit - sink)
    moved = jax.random.randint(jax.random.fold_in(key, 1), (couples,), 0, 1 << 20) % (margin + 1)
    tallies = tallies.at[1:1 + 2 * couples:2].set(source_of - moved).at[2:2 + 2 * couples:2].set(sink + moved)
    return tallies[jax.random.permutation(jax.random.fold_in(key, 2), amount)]


def gaussian(own_key, extent, scale, bound, cuts=(), kind=jnp.bfloat16):
    values = jax.random.normal(own_key, extent, jnp.float32) * scale
    if len(cuts) > 0:
        values = levels(own_key, extent, cuts, -0.22, 0.18) * values
    return jnp.clip(values, min=-bound, max=bound).astype(kind)


def setup_inputs(seed: int = 0, part: int = 0) -> dict:
    streams_of = jax.random.split(jax.random.key(seed), 14)
    part_splits = jax.random.split(jax.random.fold_in(streams_of[13], part), 14)
    query = gaussian(part_splits[0], (TOKENS, D), 1.0, 6.0, ((0, 8), (1, 2)))
    key_in = gaussian(part_splits[1], (TOKENS, D), 1.0, 6.0, ((0, 8), (1, 2)))
    value_in = gaussian(part_splits[2], (TOKENS, D), 1.0, 6.0, ((0, 8), (1, 2)))
    gate_u = gaussian(part_splits[3], (TOKENS, D), 1.0, 6.0, ((0, 8), (1, 2)))
    grad_out = gaussian(part_splits[4], (TOKENS, D), 1.0, 6.0, ((0, 8), (1, 2)))
    segment_ids = jnp.searchsorted(jnp.cumsum(uneven(part_splits[5], USERS, TOKENS, MOST, 2)), jnp.arange(TOKENS), side="right").astype(jnp.int32)
    sample_slot = draw_sample_slot(jax.random.fold_in(jax.random.fold_in(streams_of[13], part), 71), part)
    owned_input = gaussian(part_splits[7], (OWNED, D), 1.0, 6.0, ((0, 4),))
    task_grad = gaussian(part_splits[8], (OWNED, TASKS), 1.0, 6.0, ((0, 4),), jnp.float32)
    w_in = gaussian(streams_of[9], (EXPERTS, D, EH), D ** -0.5, 0.1875, ((0, 4),))
    w_out = gaussian(streams_of[10], (EXPERTS, EH, EO), EH ** -0.5, 0.25, ((0, 4),))
    w_gate = gaussian(streams_of[11], (EXPERTS, D, TASKS), D ** -0.5, 0.1875, ((0, 4),))
    tower = gaussian(streams_of[12], (TASKS, EO), 1.0, 6.0)
    return {"query": query, "key_in": key_in, "value_in": value_in, "gate_u": gate_u, "grad_out": grad_out, "segment_ids": segment_ids, "sample_slot": sample_slot, "owned_input": owned_input, "task_grad": task_grad, "w_in": w_in, "w_out": w_out, "w_gate": w_gate, "tower": tower}


def silu_slope(inputs, logistic):
    return logistic * (1.0 + inputs * (1.0 - logistic))

def expert_gradient(owned_input, task_grad, w_in, w_out, w_gate, tower):
    towers = tower.astype(jnp.float32)

    def one_expert(running, layer_set):
        first_layer, second_layer, gate_layer = layer_set
        pre_act = jnp.dot(owned_input, first_layer, preferred_element_type=jnp.float32)
        logistic = jax.nn.sigmoid(pre_act)
        activation = (pre_act * logistic).astype(jnp.bfloat16)
        expert_out = jnp.dot(activation, second_layer, preferred_element_type=jnp.float32)
        gate_prob = jax.nn.sigmoid(jnp.dot(owned_input, gate_layer, preferred_element_type=jnp.float32))
        task_score = lax.optimization_barrier(jnp.sum(expert_out[:, None, :] * towers[None, :, :], axis=2))
        weighted = task_grad * gate_prob
        grad_hidden = lax.optimization_barrier(jnp.sum(weighted[:, :, None] * towers[None, :, :], axis=1)).astype(jnp.bfloat16)
        grad_act = jnp.dot(grad_hidden, second_layer.T, preferred_element_type=jnp.float32)
        grad_pre = (grad_act * silu_slope(pre_act, logistic)).astype(jnp.bfloat16)
        grad_logit = (task_grad * task_score * gate_prob * (1.0 - gate_prob)).astype(jnp.bfloat16)
        term_sum = jnp.dot(grad_pre, first_layer.T, preferred_element_type=jnp.float32)
        term_sum = term_sum + jnp.dot(grad_logit, gate_layer.T, preferred_element_type=jnp.float32)
        return (running + term_sum, None)
    start_sum = jnp.zeros((owned_input.shape[0], owned_input.shape[1]), jnp.float32)
    running, ignored = lax.scan(one_expert, start_sum, (w_in, w_out, w_gate))
    return running.astype(jnp.bfloat16)

def block_backward(packed):
    q_part, key_part, value_part, u_part, up_part, seg_query, seg_key = packed
    n_query = q_part.shape[0]
    n_key = key_part.shape[0]
    lent_rows = n_key - n_query
    score_scale = 1.0 / math.sqrt(HDIM)
    weight_norm = 1.0 / math.sqrt(MOST)
    q_heads = q_part.reshape(n_query, HEADS, HDIM).astype(jnp.float32)
    k_heads = key_part.reshape(n_key, HEADS, HDIM).astype(jnp.float32)
    v_heads = value_part.reshape(n_key, HEADS, HDIM).astype(jnp.float32)
    u_heads = u_part.reshape(n_query, HEADS, HDIM).astype(jnp.float32)
    up_heads = up_part.reshape(n_query, HEADS, HDIM)
    query_pos = jnp.arange(n_query, dtype=jnp.int32)
    key_pos = jnp.arange(n_key, dtype=jnp.int32) - lent_rows
    visible = (seg_query[:, None] == seg_key[None, :]) & (key_pos[None, :] <= query_pos[:, None])
    scores = jnp.einsum('qhd,khd->hqk', q_heads, k_heads) * score_scale
    logistic = jax.nn.sigmoid(scores)
    weights = (jnp.where(visible[None], scores * logistic, 0.0) * weight_norm).astype(jnp.bfloat16)
    weights_wide = lax.optimization_barrier(weights).astype(jnp.float32)
    attended = jnp.einsum('hqk,khd->qhd', weights_wide, v_heads)
    grad_u = (up_heads * attended).astype(jnp.bfloat16)
    grad_attn = (up_heads * u_heads).astype(jnp.bfloat16)
    attn_wide = lax.optimization_barrier(grad_attn).astype(jnp.float32)
    grad_values = jnp.einsum('hqk,qhd->khd', weights_wide, attn_wide)
    grad_weights = jnp.einsum('qhd,khd->hqk', attn_wide, v_heads)
    grad_scores = (jnp.where(visible[None], grad_weights * silu_slope(scores, logistic), 0.0) * (score_scale * weight_norm)).astype(jnp.bfloat16)
    scores_wide = lax.optimization_barrier(grad_scores).astype(jnp.float32)
    grad_q = jnp.einsum('hqk,khd->qhd', scores_wide, k_heads).astype(jnp.bfloat16)
    grad_keys = jnp.einsum('hqk,qhd->khd', scores_wide, q_heads)
    width = HEADS * HDIM
    return (grad_q.reshape(n_query, width), grad_u.reshape(n_query, width), grad_keys.reshape(n_key, width), grad_values.reshape(n_key, width))

def reference(query, key_in, value_in, gate_u, grad_out, segment_ids, sample_slot, owned_input, task_grad, w_in, w_out, w_gate, tower):
    expert_grad = expert_gradient(owned_input, task_grad, w_in, w_out, w_gate, tower)
    row_ids = jnp.arange(TOKENS, dtype=jnp.int32)
    block_ids = row_ids // TOK_DEV
    per_owner = BLOCKS // OWNERS
    seq_ids = block_ids // per_owner
    pipe_ids = block_ids % per_owner
    slot_safe = jnp.maximum(sample_slot, 0)
    owned_row = slot_safe // SLOTS * ROWS_OWNER + (pipe_ids * OWNERS + seq_ids) * SLOTS + slot_safe % SLOTS
    picked = jnp.take(expert_grad, owned_row.astype(jnp.int32), axis=0).astype(jnp.float32)
    upstream = grad_out.astype(jnp.float32) + jnp.where(sample_slot[:, None] >= 0, picked, 0.0)
    n_blocks = TOKENS // TOK_DEV
    tail_start = TOK_DEV - MOST

    def blocks_of(whole_array):
        return whole_array.reshape((n_blocks, TOK_DEV) + whole_array.shape[1:])

    def with_tail(own_blocks, fill_value):
        previous = jnp.concatenate([jnp.full_like(own_blocks[:1, tail_start:], fill_value), own_blocks[:-1, tail_start:]], axis=0)
        return jnp.concatenate([previous, own_blocks], axis=1)
    query_blocks = blocks_of(query)
    key_blocks = blocks_of(key_in)
    value_blocks = blocks_of(value_in)
    seg_blocks = blocks_of(segment_ids)
    key_window = with_tail(key_blocks, 0)
    value_window = with_tail(value_blocks, 0)
    seg_window = with_tail(seg_blocks, -1)
    grad_q, grad_u, grad_keys, grad_values = lax.map(block_backward, (query_blocks, key_window, value_window, blocks_of(gate_u), blocks_of(upstream), seg_blocks, seg_window))

    def settle(grad_parts):
        lent_part = grad_parts[:, :MOST]
        own_part = grad_parts[:, MOST:]
        moved_back = jnp.concatenate([lent_part[1:], jnp.zeros_like(lent_part[:1])], axis=0)
        return own_part.at[:, tail_start:].add(moved_back).astype(jnp.bfloat16).reshape(TOKENS, D)
    return (grad_q.reshape(TOKENS, D), settle(grad_keys), settle(grad_values), grad_u.reshape(TOKENS, D))
```

```python
import functools
import math

import jax
import jax.numpy as jnp
from jax import lax
from jax.experimental import pallas as pl
from jax.experimental.pallas import tpu as pltpu
from jax.sharding import PartitionSpec as P

HDIM = 128
MOST = 256
TILE = 256
GATE_ROWS = 16
F32 = jnp.float32
BF16 = jnp.bfloat16
MESH = pl.DeviceIdType.MESH


def dot(a, b, ca, cb):
    return lax.dot_general(a, b, (((ca,), (cb,)), ((), ())), preferred_element_type=F32)


def logistic_of(x):
    return 0.5 * jnp.tanh(0.5 * x) + 0.5


def kernel(
    n_mp, n_seq, n_tasks,
    q_hbm, k_hbm, v_hbm, u_hbm, go_hbm, seg_ref, slot_ref, x_hbm, tg_ref,
    win_hbm, wout_hbm, wg_ref, tower_ref,
    oq, ok, ov, ou,
    q, u, go, kbuf, vbuf, x, win, wout, wg,
    slope_own, eo_own, xs, xr, xo, zs, zr,
    mask, onehot, wts, slopes, att, carry_k, carry_v, lend, back,
    lsem, xsem, wsend, wrecv, hsend, hrecv, xsend, xrecv, zsend, zrecv, bsend, brecv,
):
    seq = lax.axis_index("seq")
    mp = lax.axis_index("mp")
    pipe = lax.axis_index("pipe")
    pos = seq * 2 + pipe
    tok, feat = q.shape
    heads = feat // HDIM
    tiles = tok // TILE
    own_rows = x.shape[0]
    slot = own_rows // n_seq
    chunks = xo.shape[0]
    chunk = own_rows // chunks
    per = chunk // slot

    partner = {"pipe": 1 - pipe}
    after = {"seq": lax.rem(seq + pipe, n_seq), "pipe": 1 - pipe}
    before = {"seq": lax.rem(seq + n_seq - 1 + pipe, n_seq), "pipe": 1 - pipe}
    mp_peer = [lax.rem(mp + d, n_mp) for d in range(n_mp)]
    seq_peer = [lax.rem(seq + e, n_seq) for e in range(n_seq)]

    loads = {}
    todo = [
        ("win", win_hbm.at[0], win.at[0]),
        ("wout", wout_hbm.at[0], wout.at[0]),
        ("q", q_hbm, q),
        ("k", k_hbm, kbuf.at[pl.ds(MOST, tok)]),
        ("v", v_hbm, vbuf.at[pl.ds(MOST, tok)]),
        ("u", u_hbm, u),
        ("go", go_hbm, go),
    ]
    block_start = [
        pl.multiple_of(pipe * own_rows + seq_peer[(i + 1) % n_seq] * slot, slot)
        for i in range(n_seq)
    ]
    x_loads = [
        pltpu.make_async_copy(
            x_hbm.at[pl.ds(block_start[i], slot)], x.at[pl.ds(i * slot, slot)], xsem.at[i]
        )
        for i in range(n_seq)
    ]
    for c in x_loads:
        c.start()
    for i, (name, src, dst) in enumerate(todo):
        loads[name] = pltpu.make_async_copy(src, dst, lsem.at[i])
        loads[name].start()

    barrier = pltpu.get_barrier_semaphore()
    greet = [partner, after, before]
    greet += [{"mp": mp_peer[d]} for d in range(1, n_mp)]
    greet += [{"seq": seq_peer[e]} for e in range(1, n_seq)]
    for who in greet:
        pl.semaphore_signal(barrier, inc=1, device_id=who, device_id_type=MESH)
    pl.semaphore_wait(barrier, len(greet))

    def remote(src, dst, ssem, rsem, who):
        return pltpu.make_async_remote_copy(
            src_ref=src, dst_ref=dst, send_sem=ssem, recv_sem=rsem,
            device_id=who, device_id_type=MESH,
        )

    weights_x = [
        remote(win_hbm.at[0], win.at[1], wsend.at[0], wrecv.at[0], partner),
        remote(wout_hbm.at[0], wout.at[1], wsend.at[1], wrecv.at[1], partner),
        remote(wg_ref, wg.at[pl.ds(GATE_ROWS, GATE_ROWS)], wsend.at[2], wrecv.at[2], partner),
    ]
    for c in weights_x:
        c.start()
    halo_x = [
        remote(k_hbm.at[pl.ds(tok - MOST, MOST)], kbuf.at[pl.ds(0, MOST)],
               hsend.at[0], hrecv.at[0], after),
        remote(v_hbm.at[pl.ds(tok - MOST, MOST)], vbuf.at[pl.ds(0, MOST)],
               hsend.at[1], hrecv.at[1], after),
    ]
    for c in halo_x:
        c.start()

    wg[0:GATE_ROWS, :] = wg_ref[...]
    towers = tower_ref[...].astype(F32)

    def front(rows, e):
        pre = dot(x[rows, :], win[e], 1, 0)
        lg = logistic_of(pre)
        act = (pre * lg).astype(BF16)
        eo = dot(act, wout[e], 1, 0)
        return lg * (1.0 + pre * (1.0 - lg)), eo

    for c in x_loads:
        c.wait()
    loads["win"].wait()
    loads["wout"].wait()

    def own_front(c, _):
        rows = pl.ds(pl.multiple_of(c * chunk, chunk), chunk)
        s, e = front(rows, 0)
        slope_own[rows, :] = s
        eo_own[rows, :] = e
        return 0

    lax.fori_loop(0, chunks, own_front, 0)

    for c in weights_x:
        c.wait_recv()

    x_sends = {}
    lanes = lax.broadcasted_iota(jnp.int32, (chunk, 2 * GATE_ROWS), 1)
    for c in range(chunks):
        rows = pl.ds(c * chunk, chunk)
        tg = jnp.concatenate(
            [tg_ref[pl.ds(block_start[i], slot), :] for i in range(c * per, (c + 1) * per)], axis=0
        )
        gate = logistic_of(dot(x[rows, :], wg[...], 1, 1))
        weighted = tg * gate
        score = jnp.zeros_like(gate)
        slope_p, eo_p = front(rows, 1)
        grad_pre = []
        for e in range(2):
            eo = eo_own[rows, :] if e == 0 else eo_p
            slope = slope_own[rows, :] if e == 0 else slope_p
            hidden = 0.0
            for t in range(n_tasks):
                col = e * GATE_ROWS + t
                got = jnp.sum(eo * towers[t:t + 1, :], axis=1, keepdims=True)
                score = jnp.where(lanes == col, got, score)
                hidden = hidden + weighted[:, col:col + 1] * towers[t:t + 1, :]
            grad_act = dot(hidden.astype(BF16), wout[e], 1, 1)
            grad_pre.append((grad_act * slope).astype(BF16))
        logit = (tg * score * gate * (1.0 - gate)).astype(BF16)
        for d in list(range(1, n_mp)) + [0]:
            cols = pl.ds(pl.multiple_of(mp_peer[d] * feat, feat), feat)
            term = dot(grad_pre[0], win[0, cols, :], 1, 1)
            term = term + dot(grad_pre[1], win[1, cols, :], 1, 1)
            term = term + dot(logit, wg[:, cols], 1, 0)
            if d == 0:
                xo[c] = term
            else:
                xs[c, d - 1] = term.astype(BF16)
                x_sends[c, d] = remote(
                    xs.at[c, d - 1], xr.at[c, d - 1], xsend.at[c, d - 1], xrecv.at[c, d - 1],
                    {"mp": mp_peer[d]},
                )
                x_sends[c, d].start()

    score_scale = 1.0 / math.sqrt(HDIM)
    weight_norm = 1.0 / math.sqrt(MOST)

    seg_here = seg_ref[:, pl.ds(pl.multiple_of(pos * tok, tok), tok)]
    prev_at = pl.multiple_of(jnp.maximum(pos * tok - MOST, 0), MOST)
    seg_prev = jnp.where(pos > 0, seg_ref[:, pl.ds(prev_at, MOST)], -1)
    seg_all = jnp.concatenate([seg_prev, seg_here], axis=1)
    slot_row = slot_ref[...]
    lane128 = lax.broadcasted_iota(jnp.int32, (TILE, HDIM), 1)
    key_at = lax.broadcasted_iota(jnp.int32, (TILE, MOST + TILE), 1) - MOST
    query_at = lax.broadcasted_iota(jnp.int32, (TILE, MOST + TILE), 0)
    causal = key_at <= query_at

    def as_columns(row):
        return jnp.broadcast_to(row, (HDIM, TILE)).T

    def build(i):
        lo = i * TILE
        here = as_columns(seg_all[:, MOST + lo:MOST + lo + TILE])
        here = jnp.concatenate([here] * ((MOST + TILE) // HDIM), axis=1)
        seen = (here == seg_all[:, lo:lo + MOST + TILE]) & causal
        mask[lo:lo + TILE, :] = jnp.where(seen, weight_norm, 0.0)
        want = as_columns(slot_row[:, lo:lo + TILE])
        for b in range(own_rows // HDIM):
            onehot[lo:lo + TILE, b * HDIM:(b + 1) * HDIM] = jnp.where(
                want == lane128 + b * HDIM, 1.0, 0.0
            ).astype(BF16)

    def first_part(i):
        build(i)
        rows = pl.ds(i * TILE, TILE)
        win_rows = pl.ds(i * TILE, MOST + TILE)

        def one(h, _):
            col = pl.ds(pl.multiple_of(h * HDIM, HDIM), HDIM)
            s = dot(q[rows, col], kbuf[win_rows, col], 1, 1) * score_scale
            lg = logistic_of(s)
            sl = s * lg
            m = mask[rows, :]
            w = (sl * m).astype(BF16)
            wts[i, h] = w
            slopes[i, h] = (lg + sl * (1.0 - lg)) * (m * score_scale)
            att[rows, col] = dot(w, vbuf[win_rows, col], 1, 0)
            return 0

        lax.fori_loop(0, heads, one, 0)

    z_sends = {}

    def forward(c):
        total = xo[c]
        for d in range(1, n_mp):
            x_sends[c, d].wait_recv()
            total = total + xr[c, d - 1].astype(F32)
        zs[pl.ds(c * chunk, chunk), :] = total.astype(BF16)
        mine = pl.ds(pl.multiple_of(seq * slot, slot), slot)
        for i in range(c * per, (c + 1) * per):
            part = pl.ds(i * slot, slot)
            if i == n_seq - 1:
                zr[mine, :] = zs[part, :]
            else:
                z_sends[i] = remote(
                    zs.at[part], zr.at[mine], zsend.at[i], zrecv.at[i], {"seq": seq_peer[i + 1]}
                )
                z_sends[i].start()

    loads["q"].wait()
    loads["k"].wait()
    loads["v"].wait()
    for c in halo_x:
        c.wait_recv()
    done = 0
    for i in range(tiles):
        first_part(i)
        while done < chunks and (done + 1) * tiles <= (i + 1) * chunks * 2 - 1:
            forward(done)
            done += 1
    while done < chunks:
        forward(done)
        done += 1
    loads["u"].wait()
    loads["go"].wait()
    for i in range(n_seq - 1):
        z_sends[i].wait_recv()

    def second_part(i):
        rows = pl.ds(i * TILE, TILE)
        win_rows = pl.ds(i * TILE, MOST + TILE)

        def one(h, _):
            col = pl.ds(pl.multiple_of(h * HDIM, HDIM), HDIM)
            qh = q[rows, col]
            kh = kbuf[win_rows, col]
            vh = vbuf[win_rows, col]
            up = go[rows, col].astype(F32) + dot(onehot[rows, :], zr[:, col], 1, 0)
            ou[rows, col] = (up * att[rows, col]).astype(BF16)
            ga = (up * u[rows, col].astype(F32)).astype(BF16)
            gw = dot(ga, vh, 1, 1)
            gs = (gw * slopes[i, h]).astype(BF16)
            gv = dot(wts[i, h], ga, 0, 0)
            gk = dot(gs, qh, 0, 0)
            oq[rows, col] = dot(gs, kh, 1, 0).astype(BF16)
            if i == 0:
                lend[0, :, col] = gk[:MOST].astype(BF16)
                lend[1, :, col] = gv[:MOST].astype(BF16)
            else:
                last = pl.ds((i - 1) * TILE, TILE)
                ok[last, col] = (carry_k[:, col] + gk[:MOST]).astype(BF16)
                ov[last, col] = (carry_v[:, col] + gv[:MOST]).astype(BF16)
            carry_k[:, col] = gk[MOST:]
            carry_v[:, col] = gv[MOST:]
            return 0

        lax.fori_loop(0, heads, one, 0)

    back_x = []
    for i in range(tiles):
        second_part(i)
        if i == 0:
            for j in range(2):
                back_x.append(
                    remote(lend.at[j], back.at[j], bsend.at[j], brecv.at[j], before)
                )
                back_x[j].start()
    last = pl.ds(tok - TILE, TILE)
    back_x[0].wait_recv()
    ok[last, :] = (carry_k[...] + back[0].astype(F32)).astype(BF16)
    back_x[1].wait_recv()
    ov[last, :] = (carry_v[...] + back[1].astype(F32)).astype(BF16)
    for c in weights_x + halo_x + list(x_sends.values()) + list(z_sends.values()) + back_x:
        c.wait_send()


def shards(
    query, key_in, value_in, gate_u, grad_out, segment_ids, sample_slot,
    owned_input, task_grad, w_in, w_out, w_gate, tower,
):
    n_mp = lax.axis_size("mp")
    n_seq = lax.axis_size("seq")
    n_pipe = lax.axis_size("pipe")
    assert n_pipe == 2 and w_in.shape[0] == 1
    tok, feat = query.shape
    heads = feat // HDIM
    tiles = tok // TILE
    own_rows = owned_input.shape[0] // n_pipe
    width = owned_input.shape[1]
    hidden = w_in.shape[2]
    outs = w_out.shape[2]
    n_tasks = w_gate.shape[2]
    chunk = 256
    chunks = own_rows // chunk
    window = MOST + TILE

    gates = jnp.pad(w_gate[0].T, ((0, GATE_ROWS - n_tasks), (0, 0)))
    tg = jnp.pad(task_grad, ((0, 0), (0, GATE_ROWS - n_tasks)))
    tg = jnp.concatenate([tg, tg], axis=1)
    any_spec = pl.BlockSpec(memory_space=pl.ANY)
    vmem_spec = pl.BlockSpec(memory_space=pltpu.VMEM)
    dma = pltpu.SemaphoreType.DMA
    out = jax.ShapeDtypeStruct((tok, feat), BF16)
    return pl.pallas_call(
        functools.partial(kernel, n_mp, n_seq, n_tasks),
        out_shape=(out,) * 4,
        in_specs=[any_spec] * 5 + [vmem_spec] * 2 + [any_spec, vmem_spec]
        + [any_spec] * 2 + [vmem_spec] * 2,
        out_specs=(vmem_spec,) * 4,
        scratch_shapes=[
            pltpu.VMEM((tok, feat), BF16),
            pltpu.VMEM((tok, feat), BF16),
            pltpu.VMEM((tok, feat), BF16),
            pltpu.VMEM((tok + MOST, feat), BF16),
            pltpu.VMEM((tok + MOST, feat), BF16),
            pltpu.VMEM((own_rows, width), BF16),
            pltpu.VMEM((2, width, hidden), BF16),
            pltpu.VMEM((2, hidden, outs), BF16),
            pltpu.VMEM((2 * GATE_ROWS, width), BF16),
            pltpu.VMEM((own_rows, hidden), F32),
            pltpu.VMEM((own_rows, outs), F32),
            pltpu.VMEM((chunks, n_mp - 1, chunk, feat), BF16),
            pltpu.VMEM((chunks, n_mp - 1, chunk, feat), BF16),
            pltpu.VMEM((chunks, chunk, feat), F32),
            pltpu.VMEM((own_rows, feat), BF16),
            pltpu.VMEM((own_rows, feat), BF16),
            pltpu.VMEM((tok, window), F32),
            pltpu.VMEM((tok, own_rows), BF16),
            pltpu.VMEM((tiles, heads, TILE, window), BF16),
            pltpu.VMEM((tiles, heads, TILE, window), F32),
            pltpu.VMEM((tok, feat), F32),
            pltpu.VMEM((MOST, feat), F32),
            pltpu.VMEM((MOST, feat), F32),
            pltpu.VMEM((2, MOST, feat), BF16),
            pltpu.VMEM((2, MOST, feat), BF16),
            dma((7,)),
            dma((n_seq,)),
            dma((3,)),
            dma((3,)),
            dma((2,)),
            dma((2,)),
            dma((chunks, n_mp - 1)),
            dma((chunks, n_mp - 1)),
            dma((n_seq,)),
            dma((n_seq,)),
            dma((2,)),
            dma((2,)),
        ],
        compiler_params=pltpu.CompilerParams(
            collective_id=0, has_side_effects=True, vmem_limit_bytes=50 * 2**20
        ),
        cost_estimate=pl.CostEstimate(
            flops=6 * 2**30, bytes_accessed=16 * 2**20, transcendentals=4 * 2**20
        ),
    )(
        query, key_in, value_in, gate_u, grad_out,
        segment_ids.reshape(1, -1), sample_slot.reshape(1, -1),
        owned_input, tg, w_in, w_out, gates, tower,
    )


def solution(mesh):
    rows = P(("groups", "seq", "pipe"), "mp")
    expert = P(("mp", "pipe"), None, None)
    return jax.shard_map(
        shards,
        mesh=mesh,
        in_specs=(
            rows, rows, rows, rows, rows,
            P("groups"),
            P(("groups", "seq", "pipe")),
            P(("groups", "seq"), None),
            P(("groups", "seq"), None),
            expert, expert, expert,
            P(),
        ),
        out_specs=(rows,) * 4,
        check_vma=False,
    )
```

```python
import functools
import math

import jax
import jax.numpy as jnp
from jax import lax
from jax.experimental import pallas as pl
from jax.experimental.pallas import tpu as pltpu
from jax.sharding import PartitionSpec as P

HDIM = 128
MOST = 256
TILE = 256
GATE_ROWS = 16
F32 = jnp.float32
BF16 = jnp.bfloat16
MESH = pl.DeviceIdType.MESH


def dot(a, b, ca, cb):
    return lax.dot_general(a, b, (((ca,), (cb,)), ((), ())), preferred_element_type=F32)


def logistic_of(x):
    return 0.5 * jnp.tanh(0.5 * x) + 0.5


def kernel(
    n_mp, n_seq, n_tasks,
    q_hbm, k_hbm, v_hbm, u_hbm, go_hbm, seg_hbm, slot_hbm, x_hbm, tg_hbm,
    win_hbm, wout_hbm, gate_hbm, tower_hbm,
    oq_hbm, ok_hbm, ov_hbm, ou_hbm,
    oq, ok, ov, ou, seg_ref, slot_ref, tg_in, gate_in, tower_ref, tg_wide, tg_ref,
    q, u, go, kbuf, vbuf, x, win, wout, wg,
    slope_own, eo_own, xs, xr, xo, zs, zr,
    mask, onehot, wts, slopes, att, carry_k, carry_v, lend, back,
    lsem, xsem, wsend, wrecv, hsend, hrecv, xsend, xrecv, zsend, zrecv, bsend, brecv, osem,
):
    seq = lax.axis_index("seq")
    mp = lax.axis_index("mp")
    pipe = lax.axis_index("pipe")
    pos = seq * 2 + pipe
    tok, feat = q.shape
    heads = feat // HDIM
    tiles = tok // TILE
    own_rows = x.shape[0]
    slot = own_rows // n_seq
    chunks = xo.shape[0]
    chunk = own_rows // chunks
    per = chunk // slot

    partner = {"pipe": 1 - pipe}
    after = {"seq": lax.rem(seq + pipe, n_seq), "pipe": 1 - pipe}
    before = {"seq": lax.rem(seq + n_seq - 1 + pipe, n_seq), "pipe": 1 - pipe}
    mp_peer = [lax.rem(mp + d, n_mp) for d in range(n_mp)]
    seq_peer = [lax.rem(seq + e, n_seq) for e in range(n_seq)]

    loads = {}
    todo = [
        ("win", win_hbm.at[0], win.at[0]),
        ("wout", wout_hbm.at[0], wout.at[0]),
        ("gate", gate_hbm, gate_in),
        ("tg", tg_hbm, tg_in),
        ("tower", tower_hbm, tower_ref),
        ("seg", seg_hbm, seg_ref),
        ("slot", slot_hbm, slot_ref),
        ("q", q_hbm, q),
        ("k", k_hbm, kbuf.at[pl.ds(MOST, tok)]),
        ("v", v_hbm, vbuf.at[pl.ds(MOST, tok)]),
        ("u", u_hbm, u),
        ("go", go_hbm, go),
    ]
    block_start = [
        pl.multiple_of(pipe * own_rows + seq_peer[(i + 1) % n_seq] * slot, slot)
        for i in range(n_seq)
    ]
    block_at = [pl.multiple_of(seq_peer[(i + 1) % n_seq] * slot, slot) for i in range(n_seq)]
    x_loads = [
        pltpu.make_async_copy(
            x_hbm.at[pl.ds(block_start[i], slot)], x.at[pl.ds(i * slot, slot)], xsem.at[i]
        )
        for i in range(n_seq)
    ]
    for c in x_loads:
        c.start()
    for i, (name, src, dst) in enumerate(todo):
        loads[name] = pltpu.make_async_copy(src, dst, lsem.at[i])
        loads[name].start()

    tg_wide[...] = jnp.zeros_like(tg_wide)
    loads["gate"].wait()
    tg_wide[0:n_tasks, 0:gate_in.shape[1]] = gate_in[...].astype(F32)
    wg[0:GATE_ROWS, :] = tg_wide[0:GATE_ROWS, 0:gate_in.shape[1]].astype(BF16)

    barrier = pltpu.get_barrier_semaphore()
    greet = [partner, after, before]
    greet += [{"mp": mp_peer[d]} for d in range(1, n_mp)]
    greet += [{"seq": seq_peer[e]} for e in range(1, n_seq)]
    for who in greet:
        pl.semaphore_signal(barrier, inc=1, device_id=who, device_id_type=MESH)
    pl.semaphore_wait(barrier, len(greet))

    def remote(src, dst, ssem, rsem, who):
        return pltpu.make_async_remote_copy(
            src_ref=src, dst_ref=dst, send_sem=ssem, recv_sem=rsem,
            device_id=who, device_id_type=MESH,
        )

    weights_x = [
        remote(win_hbm.at[0], win.at[1], wsend.at[0], wrecv.at[0], partner),
        remote(wout_hbm.at[0], wout.at[1], wsend.at[1], wrecv.at[1], partner),
        remote(wg.at[pl.ds(0, GATE_ROWS)], wg.at[pl.ds(GATE_ROWS, GATE_ROWS)], wsend.at[2], wrecv.at[2], partner),
    ]
    for c in weights_x:
        c.start()
    halo_x = [
        remote(k_hbm.at[pl.ds(tok - MOST, MOST)], kbuf.at[pl.ds(0, MOST)],
               hsend.at[0], hrecv.at[0], after),
        remote(v_hbm.at[pl.ds(tok - MOST, MOST)], vbuf.at[pl.ds(0, MOST)],
               hsend.at[1], hrecv.at[1], after),
    ]
    for c in halo_x:
        c.start()

    loads["tg"].wait()
    loads["tower"].wait()
    half = tg_in[:, pl.ds(pl.multiple_of(pipe * own_rows, own_rows), own_rows)]
    tg_wide[0:n_tasks, 0:own_rows] = half
    tg_wide[GATE_ROWS:GATE_ROWS + n_tasks, 0:own_rows] = half
    tg_ref[...] = tg_wide[:, 0:own_rows].T
    towers = tower_ref[...].astype(F32)

    def front(rows, e):
        pre = dot(x[rows, :], win[e], 1, 0)
        lg = logistic_of(pre)
        act = (pre * lg).astype(BF16)
        eo = dot(act, wout[e], 1, 0)
        return lg * (1.0 + pre * (1.0 - lg)), eo

    for c in x_loads:
        c.wait()
    loads["win"].wait()
    loads["wout"].wait()

    def own_front(c, _):
        rows = pl.ds(pl.multiple_of(c * chunk, chunk), chunk)
        s, e = front(rows, 0)
        slope_own[rows, :] = s
        eo_own[rows, :] = e
        return 0

    lax.fori_loop(0, chunks, own_front, 0)

    for c in weights_x:
        c.wait_recv()

    x_sends = {}
    lanes = lax.broadcasted_iota(jnp.int32, (chunk, 2 * GATE_ROWS), 1)
    for c in range(chunks):
        rows = pl.ds(c * chunk, chunk)
        tg = jnp.concatenate(
            [tg_ref[pl.ds(block_at[i], slot), 0:2 * GATE_ROWS] for i in range(c * per, (c + 1) * per)], axis=0
        )
        gate = logistic_of(dot(x[rows, :], wg[...], 1, 1))
        weighted = tg * gate
        score = jnp.zeros_like(gate)
        slope_p, eo_p = front(rows, 1)
        grad_pre = []
        for e in range(2):
            eo = eo_own[rows, :] if e == 0 else eo_p
            slope = slope_own[rows, :] if e == 0 else slope_p
            hidden = 0.0
            for t in range(n_tasks):
                col = e * GATE_ROWS + t
                got = jnp.sum(eo * towers[t:t + 1, :], axis=1, keepdims=True)
                score = jnp.where(lanes == col, got, score)
                hidden = hidden + weighted[:, col:col + 1] * towers[t:t + 1, :]
            grad_act = dot(hidden.astype(BF16), wout[e], 1, 1)
            grad_pre.append((grad_act * slope).astype(BF16))
        logit = (tg * score * gate * (1.0 - gate)).astype(BF16)
        for d in list(range(1, n_mp)) + [0]:
            cols = pl.ds(pl.multiple_of(mp_peer[d] * feat, feat), feat)
            term = dot(grad_pre[0], win[0, cols, :], 1, 1)
            term = term + dot(grad_pre[1], win[1, cols, :], 1, 1)
            term = term + dot(logit, wg[:, cols], 1, 0)
            if d == 0:
                xo[c] = term
            else:
                xs[c, d - 1] = term.astype(BF16)
                x_sends[c, d] = remote(
                    xs.at[c, d - 1], xr.at[c, d - 1], xsend.at[c, d - 1], xrecv.at[c, d - 1],
                    {"mp": mp_peer[d]},
                )
                x_sends[c, d].start()

    score_scale = 1.0 / math.sqrt(HDIM)
    weight_norm = 1.0 / math.sqrt(MOST)

    loads["seg"].wait()
    loads["slot"].wait()
    seg_here = seg_ref[:, pl.ds(pl.multiple_of(pos * tok, tok), tok)]
    prev_at = pl.multiple_of(jnp.maximum(pos * tok - MOST, 0), MOST)
    seg_prev = jnp.where(pos > 0, seg_ref[:, pl.ds(prev_at, MOST)], -1)
    seg_all = jnp.concatenate([seg_prev, seg_here], axis=1)
    slot_row = slot_ref[...]
    lane128 = lax.broadcasted_iota(jnp.int32, (TILE, HDIM), 1)
    key_at = lax.broadcasted_iota(jnp.int32, (TILE, MOST + TILE), 1) - MOST
    query_at = lax.broadcasted_iota(jnp.int32, (TILE, MOST + TILE), 0)
    causal = key_at <= query_at

    def as_columns(row):
        return jnp.broadcast_to(row, (HDIM, TILE)).T

    def build(i):
        lo = i * TILE
        here = as_columns(seg_all[:, MOST + lo:MOST + lo + TILE])
        here = jnp.concatenate([here] * ((MOST + TILE) // HDIM), axis=1)
        seen = (here == seg_all[:, lo:lo + MOST + TILE]) & causal
        mask[lo:lo + TILE, :] = jnp.where(seen, weight_norm, 0.0)
        want = as_columns(slot_row[:, lo:lo + TILE])
        for b in range(own_rows // HDIM):
            onehot[lo:lo + TILE, b * HDIM:(b + 1) * HDIM] = jnp.where(
                want == lane128 + b * HDIM, 1.0, 0.0
            ).astype(BF16)

    def first_part(i):
        build(i)
        rows = pl.ds(i * TILE, TILE)
        win_rows = pl.ds(i * TILE, MOST + TILE)

        def one(h, _):
            col = pl.ds(pl.multiple_of(h * HDIM, HDIM), HDIM)
            s = dot(q[rows, col], kbuf[win_rows, col], 1, 1) * score_scale
            lg = logistic_of(s)
            sl = s * lg
            m = mask[rows, :]
            w = (sl * m).astype(BF16)
            wts[i, h] = w.T
            slopes[i, h] = (lg + sl * (1.0 - lg)) * (m * score_scale)
            att[rows, col] = dot(w, vbuf[win_rows, col], 1, 0)
            return 0

        lax.fori_loop(0, heads, one, 0, unroll=True)

    z_sends = {}

    def forward(c):
        total = xo[c]
        for d in range(1, n_mp):
            x_sends[c, d].wait_recv()
            total = total + xr[c, d - 1].astype(F32)
        zs[pl.ds(c * chunk, chunk), :] = total.astype(BF16)
        mine = pl.ds(pl.multiple_of(seq * slot, slot), slot)
        for i in range(c * per, (c + 1) * per):
            part = pl.ds(i * slot, slot)
            if i == n_seq - 1:
                zr[mine, :] = zs[part, :]
            else:
                z_sends[i] = remote(
                    zs.at[part], zr.at[mine], zsend.at[i], zrecv.at[i], {"seq": seq_peer[i + 1]}
                )
                z_sends[i].start()

    loads["q"].wait()
    loads["k"].wait()
    loads["v"].wait()
    for c in halo_x:
        c.wait_recv()
    forward(0)
    done = 1
    for i in range(tiles):
        first_part(i)
        if done < chunks - 1:
            forward(done)
            done += 1
    while done < chunks:
        forward(done)
        done += 1
    loads["u"].wait()
    loads["go"].wait()
    for i in range(n_seq - 1):
        z_sends[i].wait_recv()

    def second_part(i):
        rows = pl.ds(i * TILE, TILE)
        win_rows = pl.ds(i * TILE, MOST + TILE)

        def one(h, _):
            col = pl.ds(pl.multiple_of(h * HDIM, HDIM), HDIM)
            qh = q[rows, col]
            kh = kbuf[win_rows, col]
            vh = vbuf[win_rows, col]
            up = go[rows, col].astype(F32) + dot(onehot[rows, :], zr[:, col], 1, 0)
            ou[rows, col] = (up * att[rows, col]).astype(BF16)
            ga = (up * u[rows, col].astype(F32)).astype(BF16)
            gw = dot(ga, vh, 1, 1)
            gs = (gw * slopes[i, h]).astype(BF16)
            gv = dot(wts[i, h], ga, 1, 0)
            gk = dot(gs, qh, 0, 0)
            oq[rows, col] = dot(gs, kh, 1, 0).astype(BF16)
            if i == 0:
                lend[0, :, col] = gk[:MOST].astype(BF16)
                lend[1, :, col] = gv[:MOST].astype(BF16)
            else:
                last = pl.ds((i - 1) * TILE, TILE)
                ok[last, col] = (carry_k[:, col] + gk[:MOST]).astype(BF16)
                ov[last, col] = (carry_v[:, col] + gv[:MOST]).astype(BF16)
            carry_k[:, col] = gk[MOST:]
            carry_v[:, col] = gv[MOST:]
            return 0

        lax.fori_loop(0, heads, one, 0, unroll=True)

    back_x = []
    stores = []

    def store(ref, hbm, i):
        rows = pl.ds(i * TILE, TILE)
        c = pltpu.make_async_copy(ref.at[rows], hbm.at[rows], osem.at[len(stores)])
        c.start()
        stores.append(c)

    for i in range(tiles):
        second_part(i)
        store(oq, oq_hbm, i)
        store(ou, ou_hbm, i)
        if i > 0:
            store(ok, ok_hbm, i - 1)
            store(ov, ov_hbm, i - 1)
        if i == 0:
            for j in range(2):
                back_x.append(
                    remote(lend.at[j], back.at[j], bsend.at[j], brecv.at[j], before)
                )
                back_x[j].start()
    last = pl.ds(tok - TILE, TILE)
    back_x[0].wait_recv()
    ok[last, :] = (carry_k[...] + back[0].astype(F32)).astype(BF16)
    store(ok, ok_hbm, tiles - 1)
    back_x[1].wait_recv()
    ov[last, :] = (carry_v[...] + back[1].astype(F32)).astype(BF16)
    store(ov, ov_hbm, tiles - 1)
    for c in stores:
        c.wait()
    for c in weights_x + halo_x + list(x_sends.values()) + list(z_sends.values()) + back_x:
        c.wait_send()


def settle(*refs):
    count = (len(refs) - 1) // 2
    sems = refs[-1]
    copies = [
        pltpu.make_async_copy(refs[i], refs[count + i], sems.at[i]) for i in range(count)
    ]
    for c in copies:
        c.start()
    for c in copies:
        c.wait()


def shards(
    query, key_in, value_in, gate_u, grad_out, segment_ids, sample_slot,
    owned_input, task_grad, w_in, w_out, w_gate, tower,
):
    n_mp = lax.axis_size("mp")
    n_seq = lax.axis_size("seq")
    n_pipe = lax.axis_size("pipe")
    assert n_pipe == 2 and w_in.shape[0] == 1
    tok, feat = query.shape
    heads = feat // HDIM
    tiles = tok // TILE
    own_rows = owned_input.shape[0] // n_pipe
    width = owned_input.shape[1]
    hidden = w_in.shape[2]
    outs = w_out.shape[2]
    n_tasks = w_gate.shape[2]
    chunk = 128
    chunks = own_rows // chunk
    window = MOST + TILE

    any_spec = pl.BlockSpec(memory_space=pl.ANY)
    dma = pltpu.SemaphoreType.DMA
    out = jax.ShapeDtypeStruct((tok, feat), BF16)
    results = pl.pallas_call(
        functools.partial(kernel, n_mp, n_seq, n_tasks),
        out_shape=(out,) * 4,
        in_specs=[any_spec] * 13,
        out_specs=(any_spec,) * 4,
        scratch_shapes=[
            pltpu.VMEM((tok, feat), BF16),
            pltpu.VMEM((tok, feat), BF16),
            pltpu.VMEM((tok, feat), BF16),
            pltpu.VMEM((tok, feat), BF16),
            pltpu.VMEM((1, segment_ids.shape[0]), jnp.int32),
            pltpu.VMEM((1, tok), jnp.int32),
            pltpu.VMEM((n_tasks, owned_input.shape[0]), F32),
            pltpu.VMEM((n_tasks, width), BF16),
            pltpu.VMEM((n_tasks, outs), BF16),
            pltpu.VMEM((HDIM, max(own_rows, width)), F32),
            pltpu.VMEM((own_rows, HDIM), F32),
            pltpu.VMEM((tok, feat), BF16),
            pltpu.VMEM((tok, feat), BF16),
            pltpu.VMEM((tok, feat), BF16),
            pltpu.VMEM((tok + MOST, feat), BF16),
            pltpu.VMEM((tok + MOST, feat), BF16),
            pltpu.VMEM((own_rows, width), BF16),
            pltpu.VMEM((2, width, hidden), BF16),
            pltpu.VMEM((2, hidden, outs), BF16),
            pltpu.VMEM((2 * GATE_ROWS, width), BF16),
            pltpu.VMEM((own_rows, hidden), F32),
            pltpu.VMEM((own_rows, outs), F32),
            pltpu.VMEM((chunks, n_mp - 1, chunk, feat), BF16),
            pltpu.VMEM((chunks, n_mp - 1, chunk, feat), BF16),
            pltpu.VMEM((chunks, chunk, feat), F32),
            pltpu.VMEM((own_rows, feat), BF16),
            pltpu.VMEM((own_rows, feat), BF16),
            pltpu.VMEM((tok, window), F32),
            pltpu.VMEM((tok, own_rows), BF16),
            pltpu.VMEM((tiles, heads, window, TILE), BF16),
            pltpu.VMEM((tiles, heads, TILE, window), F32),
            pltpu.VMEM((tok, feat), F32),
            pltpu.VMEM((MOST, feat), F32),
            pltpu.VMEM((MOST, feat), F32),
            pltpu.VMEM((2, MOST, feat), BF16),
            pltpu.VMEM((2, MOST, feat), BF16),
            dma((12,)),
            dma((n_seq,)),
            dma((3,)),
            dma((3,)),
            dma((2,)),
            dma((2,)),
            dma((chunks, n_mp - 1)),
            dma((chunks, n_mp - 1)),
            dma((n_seq,)),
            dma((n_seq,)),
            dma((2,)),
            dma((2,)),
            dma((4 * tiles,)),
        ],
        compiler_params=pltpu.CompilerParams(
            collective_id=0, has_side_effects=True, vmem_limit_bytes=60 * 2**20
        ),
        cost_estimate=pl.CostEstimate(
            flops=6 * 2**30, bytes_accessed=16 * 2**20, transcendentals=4 * 2**20
        ),
    )(
        query, key_in, value_in, gate_u, grad_out,
        segment_ids.reshape(1, -1), sample_slot.reshape(1, -1),
        owned_input, task_grad.T, w_in, w_out, w_gate[0].T, tower,
    )
    return pl.pallas_call(
        settle,
        out_shape=(out,) * 4,
        in_specs=[any_spec] * 4,
        out_specs=(any_spec,) * 4,
        scratch_shapes=[dma((4,))],
        compiler_params=pltpu.CompilerParams(vmem_limit_bytes=60 * 2**20),
        cost_estimate=pl.CostEstimate(flops=0, bytes_accessed=8 * 2**20, transcendentals=0),
    )(*results)


def solution(mesh):
    rows = P(("groups", "seq", "pipe"), "mp")
    expert = P(("mp", "pipe"), None, None)
    return jax.shard_map(
        shards,
        mesh=mesh,
        in_specs=(
            rows, rows, rows, rows, rows,
            P("groups"),
            P(("groups", "seq", "pipe")),
            P(("groups", "seq"), None),
            P(("groups", "seq"), None),
            expert, expert, expert,
            P(),
        ),
        out_specs=(rows,) * 4,
        check_vma=False,
    )
```

```python
import functools
import math

import jax
import jax.numpy as jnp
from jax import lax
from jax.experimental import pallas as pl
from jax.experimental.pallas import tpu as pltpu
from jax.sharding import PartitionSpec as P

HDIM = 128
MOST = 256
TILE = 256
GATE_ROWS = 16
F32 = jnp.float32
BF16 = jnp.bfloat16
MESH = pl.DeviceIdType.MESH


def dot(a, b, ca, cb):
    return lax.dot_general(a, b, (((ca,), (cb,)), ((), ())), preferred_element_type=F32)


def logistic_of(x):
    return 0.5 * jnp.tanh(0.5 * x) + 0.5


def kernel(
    n_mp, n_seq, n_tasks,
    q_hbm, k_hbm, v_hbm, u_hbm, go_hbm, seg_hbm, slot_hbm, x_hbm, tg_hbm,
    win_hbm, wout_hbm, gate_hbm, tower_hbm,
    oq_hbm, ok_hbm, ov_hbm, ou_hbm,
    oq, ok, ov, ou, seg_ref, slot_ref, tg_in, gate_in, tower_ref, tg_wide, tg_ref,
    q, u, go, kbuf, vbuf, x, win, wout, wg,
    slope_own, eo_own, xs, xr, xo, zs, zr,
    mask, onehot, wts, slopes, att, carry_k, carry_v, lend, back,
    lsem, xsem, wsend, wrecv, hsend, hrecv, xsend, xrecv, zsend, zrecv, bsend, brecv, osem,
):
    seq = lax.axis_index("seq")
    mp = lax.axis_index("mp")
    pipe = lax.axis_index("pipe")
    pos = seq * 2 + pipe
    tok, feat = q.shape
    heads = feat // HDIM
    tiles = tok // TILE
    own_rows = x.shape[0]
    slot = own_rows // n_seq
    chunks = xo.shape[0]
    chunk = own_rows // chunks
    per = chunk // slot

    partner = {"pipe": 1 - pipe}
    after = {"seq": lax.rem(seq + pipe, n_seq), "pipe": 1 - pipe}
    before = {"seq": lax.rem(seq + n_seq - 1 + pipe, n_seq), "pipe": 1 - pipe}
    mp_peer = [lax.rem(mp + d, n_mp) for d in range(n_mp)]
    seq_peer = [lax.rem(seq + e, n_seq) for e in range(n_seq)]

    loads = {}
    todo = [
        ("win", win_hbm.at[0], win.at[0]),
        ("wout", wout_hbm.at[0], wout.at[0]),
        ("gate", gate_hbm, gate_in),
        ("tg", tg_hbm, tg_in),
        ("tower", tower_hbm, tower_ref),
        ("seg", seg_hbm, seg_ref),
        ("slot", slot_hbm, slot_ref),
        ("q", q_hbm, q),
        ("k", k_hbm, kbuf.at[pl.ds(MOST, tok)]),
        ("v", v_hbm, vbuf.at[pl.ds(MOST, tok)]),
        ("u", u_hbm, u),
        ("go", go_hbm, go),
    ]
    block_start = [
        pl.multiple_of(pipe * own_rows + seq_peer[(i + 1) % n_seq] * slot, slot)
        for i in range(n_seq)
    ]
    block_at = [pl.multiple_of(seq_peer[(i + 1) % n_seq] * slot, slot) for i in range(n_seq)]
    x_loads = [
        pltpu.make_async_copy(
            x_hbm.at[pl.ds(block_start[i], slot)], x.at[pl.ds(i * slot, slot)], xsem.at[i]
        )
        for i in range(n_seq)
    ]
    for c in x_loads:
        c.start()
    for i, (name, src, dst) in enumerate(todo):
        loads[name] = pltpu.make_async_copy(src, dst, lsem.at[i])
        loads[name].start()

    tg_wide[...] = jnp.zeros_like(tg_wide)
    loads["gate"].wait()
    tg_wide[0:n_tasks, 0:gate_in.shape[1]] = gate_in[...].astype(F32)
    wg[0:GATE_ROWS, :] = tg_wide[0:GATE_ROWS, 0:gate_in.shape[1]].astype(BF16)

    barrier = pltpu.get_barrier_semaphore()
    greet = [partner, after, before]
    greet += [{"mp": mp_peer[d]} for d in range(1, n_mp)]
    greet += [{"seq": seq_peer[e]} for e in range(1, n_seq)]
    for who in greet:
        pl.semaphore_signal(barrier, inc=1, device_id=who, device_id_type=MESH)
    pl.semaphore_wait(barrier, len(greet))

    def remote(src, dst, ssem, rsem, who):
        return pltpu.make_async_remote_copy(
            src_ref=src, dst_ref=dst, send_sem=ssem, recv_sem=rsem,
            device_id=who, device_id_type=MESH,
        )

    weights_x = [
        remote(win_hbm.at[0], win.at[1], wsend.at[0], wrecv.at[0], partner),
        remote(wout_hbm.at[0], wout.at[1], wsend.at[1], wrecv.at[1], partner),
        remote(wg.at[pl.ds(0, GATE_ROWS)], wg.at[pl.ds(GATE_ROWS, GATE_ROWS)], wsend.at[2], wrecv.at[2], partner),
    ]
    for c in weights_x:
        c.start()
    halo_x = [
        remote(k_hbm.at[pl.ds(tok - MOST, MOST)], kbuf.at[pl.ds(0, MOST)],
               hsend.at[0], hrecv.at[0], after),
        remote(v_hbm.at[pl.ds(tok - MOST, MOST)], vbuf.at[pl.ds(0, MOST)],
               hsend.at[1], hrecv.at[1], after),
    ]
    for c in halo_x:
        c.start()

    loads["tg"].wait()
    loads["tower"].wait()
    half = tg_in[:, pl.ds(pl.multiple_of(pipe * own_rows, own_rows), own_rows)]
    tg_wide[0:n_tasks, 0:own_rows] = half
    tg_wide[GATE_ROWS:GATE_ROWS + n_tasks, 0:own_rows] = half
    tg_ref[...] = tg_wide[:, 0:own_rows].T
    towers = tower_ref[...].astype(F32)

    def front(rows, e):
        pre = dot(x[rows, :], win[e], 1, 0)
        lg = logistic_of(pre)
        act = (pre * lg).astype(BF16)
        eo = dot(act, wout[e], 1, 0)
        return lg * (1.0 + pre * (1.0 - lg)), eo

    for c in x_loads:
        c.wait()
    loads["win"].wait()
    loads["wout"].wait()

    def own_front(c, _):
        rows = pl.ds(pl.multiple_of(c * chunk, chunk), chunk)
        s, e = front(rows, 0)
        slope_own[rows, :] = s
        eo_own[rows, :] = e
        return 0

    lax.fori_loop(0, chunks, own_front, 0)

    for c in weights_x:
        c.wait_recv()

    x_sends = {}
    lanes = lax.broadcasted_iota(jnp.int32, (chunk, 2 * GATE_ROWS), 1)
    for c in range(chunks):
        rows = pl.ds(c * chunk, chunk)
        tg = jnp.concatenate(
            [tg_ref[pl.ds(block_at[i], slot), 0:2 * GATE_ROWS] for i in range(c * per, (c + 1) * per)], axis=0
        )
        gate = logistic_of(dot(x[rows, :], wg[...], 1, 1))
        weighted = tg * gate
        score = jnp.zeros_like(gate)
        slope_p, eo_p = front(rows, 1)
        grad_pre = []
        for e in range(2):
            eo = eo_own[rows, :] if e == 0 else eo_p
            slope = slope_own[rows, :] if e == 0 else slope_p
            hidden = 0.0
            for t in range(n_tasks):
                col = e * GATE_ROWS + t
                got = jnp.sum(eo * towers[t:t + 1, :], axis=1, keepdims=True)
                score = jnp.where(lanes == col, got, score)
                hidden = hidden + weighted[:, col:col + 1] * towers[t:t + 1, :]
            grad_act = dot(hidden.astype(BF16), wout[e], 1, 1)
            grad_pre.append((grad_act * slope).astype(BF16))
        logit = (tg * score * gate * (1.0 - gate)).astype(BF16)
        for d in list(range(1, n_mp)) + [0]:
            cols = pl.ds(pl.multiple_of(mp_peer[d] * feat, feat), feat)
            term = dot(grad_pre[0], win[0, cols, :], 1, 1)
            term = term + dot(grad_pre[1], win[1, cols, :], 1, 1)
            term = term + dot(logit, wg[:, cols], 1, 0)
            if d == 0:
                xo[c] = term
            else:
                xs[c, d - 1] = term.astype(BF16)
                x_sends[c, d] = remote(
                    xs.at[c, d - 1], xr.at[c, d - 1], xsend.at[c, d - 1], xrecv.at[c, d - 1],
                    {"mp": mp_peer[d]},
                )
                x_sends[c, d].start()

    score_scale = 1.0 / math.sqrt(HDIM)
    weight_norm = 1.0 / math.sqrt(MOST)

    loads["seg"].wait()
    loads["slot"].wait()
    seg_here = seg_ref[:, pl.ds(pl.multiple_of(pos * tok, tok), tok)]
    prev_at = pl.multiple_of(jnp.maximum(pos * tok - MOST, 0), MOST)
    seg_prev = jnp.where(pos > 0, seg_ref[:, pl.ds(prev_at, MOST)], -1)
    seg_all = jnp.concatenate([seg_prev, seg_here], axis=1)
    slot_row = slot_ref[...]
    lane128 = lax.broadcasted_iota(jnp.int32, (TILE, HDIM), 1)
    key_at = lax.broadcasted_iota(jnp.int32, (TILE, MOST + TILE), 1) - MOST
    query_at = lax.broadcasted_iota(jnp.int32, (TILE, MOST + TILE), 0)
    causal = key_at <= query_at

    def as_columns(row):
        return jnp.broadcast_to(row, (HDIM, TILE)).T

    def build(i):
        lo = i * TILE
        here = as_columns(seg_all[:, MOST + lo:MOST + lo + TILE])
        here = jnp.concatenate([here] * ((MOST + TILE) // HDIM), axis=1)
        seen = (here == seg_all[:, lo:lo + MOST + TILE]) & causal
        mask[lo:lo + TILE, :] = jnp.where(seen, weight_norm, 0.0)
        want = as_columns(slot_row[:, lo:lo + TILE])
        for b in range(own_rows // HDIM):
            onehot[lo:lo + TILE, b * HDIM:(b + 1) * HDIM] = jnp.where(
                want == lane128 + b * HDIM, 1.0, 0.0
            ).astype(BF16)

    def first_part(i):
        build(i)
        rows = pl.ds(i * TILE, TILE)
        win_rows = pl.ds(i * TILE, MOST + TILE)

        def one(h, _):
            col = pl.ds(pl.multiple_of(h * HDIM, HDIM), HDIM)
            s = dot(q[rows, col], kbuf[win_rows, col], 1, 1) * score_scale
            lg = logistic_of(s)
            sl = s * lg
            m = mask[rows, :]
            w = (sl * m).astype(BF16)
            wts[i, h] = w.T
            slopes[i, h] = (lg + sl * (1.0 - lg)) * (m * score_scale)
            att[rows, col] = dot(w, vbuf[win_rows, col], 1, 0)
            return 0

        lax.fori_loop(0, heads, one, 0, unroll=True)

    z_sends = {}

    def forward(c):
        total = xo[c]
        for d in range(1, n_mp):
            x_sends[c, d].wait_recv()
            total = total + xr[c, d - 1].astype(F32)
        zs[pl.ds(c * chunk, chunk), :] = total.astype(BF16)
        mine = pl.ds(pl.multiple_of(seq * slot, slot), slot)
        for i in range(c * per, (c + 1) * per):
            part = pl.ds(i * slot, slot)
            if i == n_seq - 1:
                zr[mine, :] = zs[part, :]
            else:
                z_sends[i] = remote(
                    zs.at[part], zr.at[mine], zsend.at[i], zrecv.at[i], {"seq": seq_peer[i + 1]}
                )
                z_sends[i].start()

    loads["q"].wait()
    loads["k"].wait()
    loads["v"].wait()
    for c in halo_x:
        c.wait_recv()
    forward(0)
    done = 1
    for i in range(tiles):
        first_part(i)
        if done < chunks - 1:
            forward(done)
            done += 1
    while done < chunks:
        forward(done)
        done += 1
    loads["u"].wait()
    loads["go"].wait()
    for i in range(n_seq - 1):
        z_sends[i].wait_recv()

    def second_part(i):
        rows = pl.ds(i * TILE, TILE)
        win_rows = pl.ds(i * TILE, MOST + TILE)

        def one(h, _):
            col = pl.ds(pl.multiple_of(h * HDIM, HDIM), HDIM)
            qh = q[rows, col]
            kh = kbuf[win_rows, col]
            vh = vbuf[win_rows, col]
            up = go[rows, col].astype(F32) + dot(onehot[rows, :], zr[:, col], 1, 0)
            ou[rows, col] = (up * att[rows, col]).astype(BF16)
            ga = (up * u[rows, col].astype(F32)).astype(BF16)
            gw = dot(ga, vh, 1, 1)
            gs = (gw * slopes[i, h]).astype(BF16)
            gv = dot(wts[i, h], ga, 1, 0)
            gk = dot(gs, qh, 0, 0)
            oq[rows, col] = dot(gs, kh, 1, 0).astype(BF16)
            if i == 0:
                lend[0, :, col] = gk[:MOST].astype(BF16)
                lend[1, :, col] = gv[:MOST].astype(BF16)
            else:
                last = pl.ds((i - 1) * TILE, TILE)
                ok[last, col] = (carry_k[:, col] + gk[:MOST]).astype(BF16)
                ov[last, col] = (carry_v[:, col] + gv[:MOST]).astype(BF16)
            carry_k[:, col] = gk[MOST:]
            carry_v[:, col] = gv[MOST:]
            return 0

        lax.fori_loop(0, heads, one, 0, unroll=True)

    back_x = []
    stores = []

    def store(ref, hbm, i):
        rows = pl.ds(i * TILE, TILE)
        c = pltpu.make_async_copy(ref.at[rows], hbm.at[rows], osem.at[len(stores)])
        c.start()
        stores.append(c)

    for i in range(tiles):
        second_part(i)
        store(oq, oq_hbm, i)
        store(ou, ou_hbm, i)
        if i > 0:
            store(ok, ok_hbm, i - 1)
            store(ov, ov_hbm, i - 1)
        if i == 0:
            for j in range(2):
                back_x.append(
                    remote(lend.at[j], back.at[j], bsend.at[j], brecv.at[j], before)
                )
                back_x[j].start()
    last = pl.ds(tok - TILE, TILE)
    back_x[0].wait_recv()
    ok[last, :] = (carry_k[...] + back[0].astype(F32)).astype(BF16)
    store(ok, ok_hbm, tiles - 1)
    back_x[1].wait_recv()
    ov[last, :] = (carry_v[...] + back[1].astype(F32)).astype(BF16)
    store(ov, ov_hbm, tiles - 1)
    for c in stores:
        c.wait()
    for c in weights_x + halo_x + list(x_sends.values()) + list(z_sends.values()) + back_x:
        c.wait_send()


def settle(*refs):
    count = (len(refs) - 3) // 2
    held, load_sem, store_sem = refs[-3:]
    parts = load_sem.shape[1]
    rows = held.shape[1] // parts
    every = [(i, pl.ds(j * rows, rows), j) for j in range(parts) for i in range(count)]
    loads = [
        pltpu.make_async_copy(refs[i].at[part], held.at[i, part], load_sem.at[i, j])
        for i, part, j in every
    ]
    stores = [
        pltpu.make_async_copy(held.at[i, part], refs[count + i].at[part], store_sem.at[i, j])
        for i, part, j in every
    ]
    for c in loads:
        c.start()
    for load, store in zip(loads, stores):
        load.wait()
        store.start()
    for c in stores:
        c.wait()


def shards(
    query, key_in, value_in, gate_u, grad_out, segment_ids, sample_slot,
    owned_input, task_grad, w_in, w_out, w_gate, tower,
):
    n_mp = lax.axis_size("mp")
    n_seq = lax.axis_size("seq")
    n_pipe = lax.axis_size("pipe")
    assert n_pipe == 2 and w_in.shape[0] == 1
    tok, feat = query.shape
    heads = feat // HDIM
    tiles = tok // TILE
    own_rows = owned_input.shape[0] // n_pipe
    width = owned_input.shape[1]
    hidden = w_in.shape[2]
    outs = w_out.shape[2]
    n_tasks = w_gate.shape[2]
    chunk = 128
    chunks = own_rows // chunk
    window = MOST + TILE

    any_spec = pl.BlockSpec(memory_space=pl.ANY)
    dma = pltpu.SemaphoreType.DMA
    out = jax.ShapeDtypeStruct((tok, feat), BF16)
    results = pl.pallas_call(
        functools.partial(kernel, n_mp, n_seq, n_tasks),
        out_shape=(out,) * 4,
        in_specs=[any_spec] * 13,
        out_specs=(any_spec,) * 4,
        scratch_shapes=[
            pltpu.VMEM((tok, feat), BF16),
            pltpu.VMEM((tok, feat), BF16),
            pltpu.VMEM((tok, feat), BF16),
            pltpu.VMEM((tok, feat), BF16),
            pltpu.VMEM((1, segment_ids.shape[0]), jnp.int32),
            pltpu.VMEM((1, tok), jnp.int32),
            pltpu.VMEM((n_tasks, owned_input.shape[0]), F32),
            pltpu.VMEM((n_tasks, width), BF16),
            pltpu.VMEM((n_tasks, outs), BF16),
            pltpu.VMEM((HDIM, max(own_rows, width)), F32),
            pltpu.VMEM((own_rows, HDIM), F32),
            pltpu.VMEM((tok, feat), BF16),
            pltpu.VMEM((tok, feat), BF16),
            pltpu.VMEM((tok, feat), BF16),
            pltpu.VMEM((tok + MOST, feat), BF16),
            pltpu.VMEM((tok + MOST, feat), BF16),
            pltpu.VMEM((own_rows, width), BF16),
            pltpu.VMEM((2, width, hidden), BF16),
            pltpu.VMEM((2, hidden, outs), BF16),
            pltpu.VMEM((2 * GATE_ROWS, width), BF16),
            pltpu.VMEM((own_rows, hidden), F32),
            pltpu.VMEM((own_rows, outs), F32),
            pltpu.VMEM((chunks, n_mp - 1, chunk, feat), BF16),
            pltpu.VMEM((chunks, n_mp - 1, chunk, feat), BF16),
            pltpu.VMEM((chunks, chunk, feat), F32),
            pltpu.VMEM((own_rows, feat), BF16),
            pltpu.VMEM((own_rows, feat), BF16),
            pltpu.VMEM((tok, window), F32),
            pltpu.VMEM((tok, own_rows), BF16),
            pltpu.VMEM((tiles, heads, window, TILE), BF16),
            pltpu.VMEM((tiles, heads, TILE, window), F32),
            pltpu.VMEM((tok, feat), F32),
            pltpu.VMEM((MOST, feat), F32),
            pltpu.VMEM((MOST, feat), F32),
            pltpu.VMEM((2, MOST, feat), BF16),
            pltpu.VMEM((2, MOST, feat), BF16),
            dma((12,)),
            dma((n_seq,)),
            dma((3,)),
            dma((3,)),
            dma((2,)),
            dma((2,)),
            dma((chunks, n_mp - 1)),
            dma((chunks, n_mp - 1)),
            dma((n_seq,)),
            dma((n_seq,)),
            dma((2,)),
            dma((2,)),
            dma((4 * tiles,)),
        ],
        compiler_params=pltpu.CompilerParams(
            collective_id=0, has_side_effects=True, vmem_limit_bytes=60 * 2**20
        ),
        cost_estimate=pl.CostEstimate(
            flops=6 * 2**30, bytes_accessed=16 * 2**20, transcendentals=4 * 2**20
        ),
    )(
        query, key_in, value_in, gate_u, grad_out,
        segment_ids.reshape(1, -1), sample_slot.reshape(1, -1),
        owned_input, task_grad.T, w_in, w_out, w_gate[0].T, tower,
    )
    return pl.pallas_call(
        settle,
        out_shape=(out,) * 4,
        in_specs=[any_spec] * 4,
        out_specs=(any_spec,) * 4,
        scratch_shapes=[pltpu.VMEM((4, tok, feat), BF16), dma((4, 2)), dma((4, 2))],
        compiler_params=pltpu.CompilerParams(vmem_limit_bytes=60 * 2**20),
        cost_estimate=pl.CostEstimate(flops=0, bytes_accessed=8 * 2**20, transcendentals=0),
    )(*results)


def solution(mesh):
    rows = P(("groups", "seq", "pipe"), "mp")
    expert = P(("mp", "pipe"), None, None)
    return jax.shard_map(
        shards,
        mesh=mesh,
        in_specs=(
            rows, rows, rows, rows, rows,
            P("groups"),
            P(("groups", "seq", "pipe")),
            P(("groups", "seq"), None),
            P(("groups", "seq"), None),
            expert, expert, expert,
            P(),
        ),
        out_specs=(rows,) * 4,
        check_vma=False,
    )
```
